256 devices in a mesh: loop: 32 (over x_lo, z, core), row: 8 (over x_hi, y).
Axes of the slice: x: 4 (x_hi: 2, x_lo: 2; x = x_hi * 2 + x_lo), y: 4, z: 8, core: 2. Of those that a mesh axis runs over, the one named last changes fastest.
Arguments:
- start_pos: int32 [32], replicated, may hold values from 0 to 31, each once
- field_noise: float32 [32, 16, 256], replicated, may hold values from -5 to 5
- green_half: bfloat16 [512, 200, 1600], P('loop', None, 'row'), may hold values from -6 to 6
- orbitals: bfloat16 [512, 1600, 200], P('loop', 'row'), may hold values from -6 to 6
- rotated: bfloat16 [256, 200, 1600], P('loop', None, 'row'), may hold values from -0.009765625 to 0.009765625
- factors: bfloat16 [256, 1600, 1600], P('loop', 'row'), may hold values from -0.0546875 to 0.0546875
Outputs:
- propagated: float32 [512, 1600, 200], P('loop', 'row')
The draws below stay inside these ranges and needn't reach their ends.
Inputs may be any that keep to these rules, and one draw needn't show every extreme that they name: `start_pos`: every loop position is the starting position of exactly one walker block.
All inputs are finite; a program needn't handle non-finite values.
Results may differ from the reference program's by a relative error of at most 0.0041.
Values may be sent and summed in bfloat16 or wider, within the bound.
A program may use at most 128 MiB of HBM per device.

```python
import jax
import jax.numpy as jnp
from jax import lax

NORB = 1600
NOCC = 200
VEC_DEV = 8
BLOCK = 16
NVEC = 256
WALKERS = 512
N_LOOP = 32


def block_levels(own_key, shape, split, smallest, high):
    level, own = 1.0, jax.random.fold_in(own_key, 6)
    for dim, shards_of in split:
        draws = jnp.exp(jax.random.uniform(jax.random.fold_in(own, dim), (shards_of,), jnp.float32, smallest / len(split), high / len(split)))
        level = level * jnp.repeat(draws, shape[dim] // shards_of).reshape([-1 if axis == dim else 1 for axis in range(len(shape))])
    return level


def noise(key, shape, deviation, reach, split=(), held_as=jnp.bfloat16):
    array = deviation * jax.random.normal(key, shape, jnp.float32)
    if split:
        array = array * block_levels(key, shape, split, -0.22, 0.18)
    return jnp.clip(array, -reach, reach).astype(held_as)


def setup_inputs(seed: int = 0) -> dict:
    arg_keys = jax.random.split(jax.random.key(seed), 7)
    return {
        "start_pos": jax.random.permutation(arg_keys[0], N_LOOP).astype(jnp.int32),
        "field_noise": noise(arg_keys[1], (N_LOOP, BLOCK, NVEC), 1.0, 5.0, (), jnp.float32),
        "green_half": noise(arg_keys[2], (WALKERS, NOCC, NORB), 1.0, 6.0, ((0, 32), (2, 8))),
        "orbitals": noise(arg_keys[3], (WALKERS, NORB, NOCC), 1.0, 6.0, ((0, 32), (1, 8))),
        "rotated": noise(arg_keys[4], (NVEC, NOCC, NORB), (NOCC * NORB) ** -0.5, 0.009765625, ((0, 32), (2, 8))),
        "factors": noise(arg_keys[5], (NVEC, NORB, NORB), (NORB * VEC_DEV) ** -0.5, 0.0546875, ((0, 32), (1, 8))),
    }


def reference(start_pos, field_noise, green_half, orbitals, rotated, factors):
    block_of = jnp.zeros((N_LOOP,), jnp.int32).at[start_pos].set(jnp.arange(N_LOOP, dtype=jnp.int32))

    def one_position(position):
        green = lax.dynamic_slice_in_dim(green_half, position * BLOCK, BLOCK, 0).astype(jnp.float32)
        orbit = lax.dynamic_slice_in_dim(orbitals, position * BLOCK, BLOCK, 0).astype(jnp.float32)
        noise_table = lax.dynamic_index_in_dim(field_noise, block_of[position], 0, keepdims=False)
        total = jnp.zeros((BLOCK, NORB, NOCC), jnp.float32)
        for stop in range(2):
            group = ((position + stop) % N_LOOP).astype(jnp.int32)
            rot_group = lax.dynamic_slice_in_dim(rotated, group * VEC_DEV, VEC_DEV, 0).astype(jnp.float32)
            fac_group = lax.dynamic_slice_in_dim(factors, group * VEC_DEV, VEC_DEV, 0).astype(jnp.float32)
            force_bias = jnp.einsum("wip,gip->wg", green, rot_group)
            noise_part = lax.dynamic_slice_in_dim(noise_table, group * VEC_DEV, VEC_DEV, 1)
            shifted = lax.optimization_barrier((noise_part - force_bias).astype(jnp.bfloat16))
            operator = jnp.einsum("wg,gpr->wpr", shifted.astype(jnp.float32), fac_group)
            operator = lax.optimization_barrier(operator.astype(jnp.bfloat16))
            total = total + jnp.einsum("wpr,wrn->wpn", operator.astype(jnp.float32), orbit)
        return total

    result = lax.map(one_position, jnp.arange(N_LOOP, dtype=jnp.int32))
    return result.reshape(N_LOOP * BLOCK, NORB, NOCC)
```

```python
import functools

import jax
import jax.numpy as jnp
from jax import lax
from jax.experimental import pallas as pl
from jax.experimental.pallas import tpu as pltpu
from jax.sharding import PartitionSpec as P

MESH = pl.DeviceIdType.MESH
F32, BF16 = jnp.float32, jnp.bfloat16
EXACT = lax.Precision.HIGHEST
LANE, TILE = 128, 16
SPLIT = (9, 4, 8, 4)
FAC_CUTS = (0, 512, 1024, 1536, 1600)
SHARD_ORDER = ((0, 0), (0, 1), (0, 3), (1, 0), (0, 2), (1, 1), (1, 3), (1, 2))


def same_slot(rows, cols, width):
    row = lax.broadcasted_iota(jnp.int32, (rows, cols), 0)
    col = lax.broadcasted_iota(jnp.int32, (rows, cols), 1)
    return lax.rem(row, width) == lax.rem(col, width)


def group_sum(rows, width):
    row = lax.broadcasted_iota(jnp.int32, (rows, LANE), 0)
    col = lax.broadcasted_iota(jnp.int32, (rows, LANE), 1)
    return (row // width == col // TILE).astype(F32)


def exact_dot(a, b):
    return lax.dot_general(a, b, (((1,), (0,)), ((), ())), precision=EXACT, preferred_element_type=F32)


def partial_bias(green, rot):
    walkers, nocc, width = green.shape
    vecs = rot.shape[0]
    whole = nocc // TILE
    left = nocc - whole * TILE

    def step(block, total):
        rows = pl.ds(pl.multiple_of(block * TILE, TILE), TILE)
        a = green[:, rows, :].reshape(walkers * TILE, width)
        b = rot[:, rows, :].reshape(vecs * TILE, width)
        return total + lax.dot_general(a, b, (((1,), (1,)), ((), ())), preferred_element_type=F32)

    total = lax.fori_loop(0, whole, step, jnp.zeros((walkers * TILE, vecs * TILE), F32))
    total = jnp.where(same_slot(walkers * TILE, vecs * TILE, TILE), total, 0.0)
    bias = exact_dot(total.reshape(walkers, TILE, vecs * TILE).sum(1), group_sum(vecs * TILE, TILE))
    if left:
        a = green[:, whole * TILE :, :].astype(F32).reshape(walkers * left, width).astype(BF16)
        b = rot[:, whole * TILE :, :].astype(F32).reshape(vecs * left, width).astype(BF16)
        rest = lax.dot_general(a, b, (((1,), (1,)), ((), ())), preferred_element_type=F32)
        rest = jnp.where(same_slot(walkers * left, vecs * left, left), rest, 0.0)
        bias += exact_dot(rest.reshape(walkers, left, vecs * left).sum(1), group_sum(vecs * left, left))
    return bias


def kernel(
    peers, start_pos, noise, green, orb, rot, fac, out,
    buf, orb_own, green_own, green_in, rot_own, fac_own, fac_in, oper, mix, mix_left, part, bias,
    own_sem, ag_send, ag_recv, fac_send, fac_recv, green_sem, bias_send, bias_recv,
):
    walkers, nrow, nocc = orb_own.shape
    vecs = rot_own.shape[0]
    l, r = lax.axis_index("loop"), lax.axis_index("row")
    half, y = r // 4, lax.rem(r, 4)

    def row(h, step):
        return lax.rem(half + h, 2) * 4 + lax.rem(y + step, 4)

    before, after = lax.rem(l + peers - 1, peers), lax.rem(l + 1, peers)
    up, down, across = (l, row(0, 1)), (l, row(0, 3)), (l, row(1, 0))

    loads = [
        pltpu.make_async_copy(src, dst, own_sem.at[i])
        for i, (src, dst) in enumerate(
            ((orb, orb_own), (green, green_own), (rot, rot_own), (fac, fac_own))
        )
    ]
    for load in loads:
        load.start()

    barrier = pltpu.get_barrier_semaphore()
    for d in range(1, 8):
        pl.semaphore_signal(barrier, inc=1, device_id=(l, lax.rem(r + d, 8)), device_id_type=MESH)
    for d in range(8):
        pl.semaphore_signal(barrier, inc=1, device_id=(after, lax.rem(r + d, 8)), device_id_type=MESH)
    pl.semaphore_signal(barrier, inc=1, device_id=(before, r), device_id_type=MESH)

    loads[0].wait()
    for w in range(walkers):
        buf[r, :, w * nocc : (w + 1) * nocc] = orb_own[w]
    pl.semaphore_wait(barrier, 16)

    sends = []

    def send(src, dst, send_sem, recv_sem, target):
        copy = pltpu.make_async_remote_copy(
            src_ref=src, dst_ref=dst, send_sem=send_sem, recv_sem=recv_sem,
            device_id=target, device_id_type=MESH,
        )
        copy.start()
        sends.append(copy)
        return copy

    a1, a2, b1, b2 = SPLIT
    pieces = {
        "A1": (0, a1), "A2": (a1, a2), "A": (0, a1 + a2),
        "B1": (a1 + a2, b1), "B2": (a1 + a2 + b1, b2), "B": (a1 + a2, b1 + b2),
    }
    used = [0]

    def pass_on(origin, piece, target):
        i = used[0]
        used[0] += 1
        first, count = pieces[piece]
        ref = buf.at[origin, :, pl.ds(first * LANE, count * LANE)]
        return send(ref, ref, ag_send.at[i], ag_recv.at[i], target)

    up_a, down_b = pass_on(r, "A", up), pass_on(r, "B", down)
    across_a, across_b = pass_on(r, "A", across), pass_on(r, "B", across)
    up_b, down_a = pass_on(r, "B", up), pass_on(r, "A", down)
    green_copy = send(green, green_in, green_sem.at[0], green_sem.at[1], (after, r))
    fac_copies = []
    for i in range(len(FAC_CUTS) - 1):
        cut = pl.ds(FAC_CUTS[i], FAC_CUTS[i + 1] - FAC_CUTS[i])
        fac_copies.append(
            send(fac.at[:, :, cut], fac_in.at[:, :, cut], fac_send.at[i], fac_recv.at[i], (before, r))
        )

    loads[1].wait()
    loads[2].wait()
    part[0] = partial_bias(green_own, rot_own)
    bias[0, r] = part[0]
    for d in range(1, 8):
        send(part.at[0], bias.at[0, r], bias_send.at[0, d], bias_recv.at[0, r], (l, lax.rem(r + d, 8)))

    up_a.wait_recv()
    pass_2 = pass_on(row(0, 3), "A2", up), pass_on(row(0, 3), "A1", up)
    pass_2x = pass_on(row(0, 3), "A1", across), pass_on(row(0, 3), "A2", across)
    down_b.wait_recv()
    pass_3 = pass_on(row(0, 1), "B2", down), pass_on(row(0, 1), "B1", down)
    pass_3x = pass_on(row(0, 1), "B1", across), pass_on(row(0, 1), "B2", across)
    across_a.wait_recv()
    pass_4m = pass_on(row(1, 0), "A", down)
    across_b.wait_recv()
    pass_4p = pass_on(row(1, 0), "B", up)

    green_copy.wait_recv()
    part[1] = partial_bias(green_in, rot_own)
    for d in range(8):
        send(part.at[1], bias.at[1, r], bias_send.at[1, d], bias_recv.at[1, r], (before, lax.rem(r + d, 8)))

    block = jnp.int32(0)
    for k in range(peers):
        block = jnp.where(start_pos[k] == l, jnp.int32(k), block)
    table = noise[block]
    columns = table.shape[1]
    row_id = lax.broadcasted_iota(jnp.int32, (columns, 2 * vecs * TILE), 0)
    col_id = lax.broadcasted_iota(jnp.int32, (columns, 2 * vecs * TILE), 1)
    pick = (row_id == lax.rem(l * vecs + col_id // TILE, columns)).astype(F32)
    noise_part = exact_dot(table, pick)

    pass_2x[0].wait_recv()
    pass_5 = pass_on(row(1, 3), "A1", up)
    pass_3x[0].wait_recv()
    pass_6 = pass_on(row(1, 1), "B1", down)
    pass_2[0].wait_recv()
    pass_7a = pass_on(row(0, 2), "A2", across)
    pass_3[0].wait_recv()
    pass_7b = pass_on(row(0, 2), "B2", across)

    for s in range(2):
        for d in range(1 - s, 8):
            j = lax.rem(r + d, 8)
            pltpu.make_async_remote_copy(
                src_ref=part.at[s], dst_ref=bias.at[s, j], send_sem=bias_send.at[s, d],
                recv_sem=bias_recv.at[s, j], device_id=across, device_id_type=MESH,
            ).wait_recv()
    sums = []
    for s in range(2):
        total = bias[s, 0]
        for j in range(1, 8):
            total += bias[s, j]
        sums.append(total)
    shifted = (noise_part - jnp.concatenate(sums, axis=1)).astype(BF16).astype(F32)
    depth = 2 * vecs * TILE
    spread = jnp.broadcast_to(shifted[:, None, :], (walkers, TILE, depth)).reshape(walkers * TILE, depth)
    mix[...] = jnp.where(same_slot(walkers * TILE, depth, TILE), spread, 0.0).astype(BF16)
    whole = nrow // TILE
    left = nrow - whole * TILE
    if left:
        row_id = lax.broadcasted_iota(jnp.int32, (depth, 2 * vecs * left), 0)
        col_id = lax.broadcasted_iota(jnp.int32, (depth, 2 * vecs * left), 1)
        few = exact_dot(shifted, (row_id == col_id // left * TILE).astype(F32))
        spread = jnp.broadcast_to(few[:, None, :], (walkers, left, 2 * vecs * left))
        spread = spread.reshape(walkers * left, 2 * vecs * left)
        mix_left[...] = jnp.where(same_slot(walkers * left, 2 * vecs * left, left), spread, 0.0).astype(BF16)

    def operator_of(shard):
        lanes = slice(shard * nrow, (shard + 1) * nrow)

        @pl.loop(0, whole)
        def _(block):
            rows = pl.ds(pl.multiple_of(block * TILE, TILE), TILE)
            both = jnp.concatenate(
                [f[:, rows, lanes].reshape(vecs * TILE, nrow) for f in (fac_own, fac_in)], axis=0
            )
            result = jnp.dot(mix[...], both, preferred_element_type=F32).astype(BF16)
            oper[shard, :, rows, :] = result.reshape(walkers, TILE, nrow)

        if left:
            rows = slice(whole * TILE, nrow)
            both = jnp.concatenate(
                [f[:, rows, lanes].astype(F32).reshape(vecs * left, nrow) for f in (fac_own, fac_in)], axis=0
            ).astype(BF16)
            result = jnp.dot(mix_left[...], both, preferred_element_type=F32)
            oper[shard, :, rows, :] = result.reshape(walkers, left, nrow).astype(BF16)

    loads[3].wait()
    done = 0
    for i, copy in enumerate(fac_copies):
        copy.wait_recv()
        while done < 8 and (done + 1) * nrow <= FAC_CUTS[i + 1]:
            operator_of(done)
            done += 1

    def apply(shard, first):
        for w in range(walkers):
            product = jnp.dot(
                oper[shard, w, 0:nrow, :],
                buf[shard, :, w * nocc : (w + 1) * nocc],
                preferred_element_type=F32,
            )
            out[w] = product if first else out[w] + product

    apply(r, True)
    for copy in (up_b, down_a, *pass_2[1:], *pass_3[1:], pass_4m, pass_4p, *pass_2x[1:], *pass_3x[1:]):
        copy.wait_recv()

    @pl.loop(1, 7)
    def _(step):
        over = step // 4
        along = lax.rem(step, 4) + step // 6
        apply(row(over, along), False)

    for copy in (pass_5, pass_6, pass_7a, pass_7b):
        copy.wait_recv()
    apply(row(1, 2), False)
    for copy in sends:
        copy.wait_send()


def body(start_pos, field_noise, green_half, orbitals, rotated, factors):
    peers = lax.axis_size("loop")
    walkers, nrow, nocc = orbitals.shape
    vecs, _, norb = factors.shape
    width = green_half.shape[2]
    left = nrow % TILE
    dma = pltpu.SemaphoreType.DMA
    vmem, hbm = pl.BlockSpec(memory_space=pltpu.VMEM), pl.BlockSpec(memory_space=pl.ANY)
    return pl.pallas_call(
        functools.partial(kernel, peers),
        out_shape=jax.ShapeDtypeStruct((walkers, nrow, nocc), F32),
        in_specs=[pl.BlockSpec(memory_space=pltpu.SMEM), vmem, hbm, hbm, hbm, hbm],
        out_specs=vmem,
        scratch_shapes=[
            pltpu.VMEM((8, nrow, walkers * nocc), BF16),
            pltpu.VMEM((walkers, nrow, nocc), BF16),
            pltpu.VMEM((walkers, nocc, width), BF16),
            pltpu.VMEM((walkers, nocc, width), BF16),
            pltpu.VMEM((vecs, nocc, width), BF16),
            pltpu.VMEM((vecs, nrow, norb), BF16),
            pltpu.VMEM((vecs, nrow, norb), BF16),
            pltpu.VMEM((8, walkers, nrow, nrow), BF16),
            pltpu.VMEM((walkers * TILE, 2 * vecs * TILE), BF16),
            pltpu.VMEM((walkers * left, 2 * vecs * left), BF16),
            pltpu.VMEM((2, walkers, LANE), F32),
            pltpu.VMEM((2, 8, walkers, LANE), F32),
            dma((4,)),
            dma((24,)),
            dma((24,)),
            dma((4,)),
            dma((4,)),
            dma((2,)),
            dma((2, 8)),
            dma((2, 8)),
        ],
        compiler_params=pltpu.CompilerParams(
            collective_id=0, has_side_effects=True, vmem_limit_bytes=60 * 2**20
        ),
        cost_estimate=pl.CostEstimate(
            flops=8 * walkers * nrow * norb * nocc, bytes_accessed=2 * 10**7, transcendentals=0
        ),
    )(start_pos, field_noise, green_half, orbitals, rotated, factors)


def solution(mesh):
    return jax.shard_map(
        body,
        mesh=mesh,
        in_specs=(
            P(),
            P(),
            P("loop", None, "row"),
            P("loop", "row", None),
            P("loop", None, "row"),
            P("loop", "row", None),
        ),
        out_specs=P("loop", "row", None),
        check_vma=False,
    )
```

```python
import functools

import jax
import jax.numpy as jnp
from jax import lax
from jax.experimental import pallas as pl
from jax.experimental.pallas import tpu as pltpu
from jax.sharding import PartitionSpec as P

MESH = pl.DeviceIdType.MESH
F32, BF16 = jnp.float32, jnp.bfloat16
EXACT = lax.Precision.HIGHEST
LANE, TILE = 128, 16
PARTS = 4
RELAY_Z = (0, 3, 4)


def same_slot(rows, cols, width):
    row = lax.broadcasted_iota(jnp.int32, (rows, cols), 0)
    col = lax.broadcasted_iota(jnp.int32, (rows, cols), 1)
    return lax.rem(row, width) == lax.rem(col, width)


def group_sum(rows, width):
    row = lax.broadcasted_iota(jnp.int32, (rows, LANE), 0)
    col = lax.broadcasted_iota(jnp.int32, (rows, LANE), 1)
    return (row // width == col // TILE).astype(F32)


def exact_dot(a, b):
    return lax.dot_general(a, b, (((1,), (0,)), ((), ())), precision=EXACT, preferred_element_type=F32)


def partial_bias(green, rot):
    walkers, nocc, width = green.shape
    vecs = rot.shape[0]
    whole = nocc // TILE
    left = nocc - whole * TILE

    def step(block, total):
        rows = pl.ds(pl.multiple_of(block * TILE, TILE), TILE)
        a = green[:, rows, :].reshape(walkers * TILE, width)
        b = rot[:, rows, :].reshape(vecs * TILE, width)
        return total + lax.dot_general(a, b, (((1,), (1,)), ((), ())), preferred_element_type=F32)

    total = lax.fori_loop(0, whole, step, jnp.zeros((walkers * TILE, vecs * TILE), F32))
    total = jnp.where(same_slot(walkers * TILE, vecs * TILE, TILE), total, 0.0)
    bias = exact_dot(total.reshape(walkers, TILE, vecs * TILE).sum(1), group_sum(vecs * TILE, TILE))
    if left:
        a = green[:, whole * TILE :, :].astype(F32).reshape(walkers * left, width).astype(BF16)
        b = rot[:, whole * TILE :, :].astype(F32).reshape(vecs * left, width).astype(BF16)
        rest = lax.dot_general(a, b, (((1,), (1,)), ((), ())), preferred_element_type=F32)
        rest = jnp.where(same_slot(walkers * left, vecs * left, left), rest, 0.0)
        bias += exact_dot(rest.reshape(walkers, left, vecs * left).sum(1), group_sum(vecs * left, left))
    return bias


def kernel(
    peers, start_pos, noise, green, orb, rot, fac, out,
    buf, orb_own, green_own, green_in, rot_own, fac_own, fac_in, fac_relay, oper, mix, mix_left, part, bias,
    own_sem, ag_send, ag_recv, fac_send, fac_recv, relay_sem, green_sem, bias_send, bias_recv,
):
    walkers, nrow, nocc = orb_own.shape
    vecs = rot_own.shape[0]
    l, r = lax.axis_index("loop"), lax.axis_index("row")
    half, y = r // 4, lax.rem(r, 4)

    def row(h, step):
        return lax.rem(half + h, 2) * 4 + lax.rem(y + step, 4)

    before, after = lax.rem(l + peers - 1, peers), lax.rem(l + 1, peers)
    up, down, across = (l, row(0, 1)), (l, row(0, 3)), (l, row(1, 0))

    turn = peers // 2
    near, far = (l // turn) * turn, lax.rem((l // turn) * turn + turn, peers)
    place = lax.rem(l, turn)
    is_source, is_last = place == 0, place == turn - 1
    is_relay = functools.reduce(jnp.logical_or, [place == 2 * z for z in RELAY_Z])

    loads = [
        pltpu.make_async_copy(src, dst, own_sem.at[i])
        for i, (src, dst) in enumerate(
            ((orb, orb_own), (green, green_own), (rot, rot_own), (fac, fac_own))
        )
    ]
    for load in loads:
        load.start()

    barrier = pltpu.get_barrier_semaphore()
    for d in range(1, 8):
        pl.semaphore_signal(barrier, inc=1, device_id=(l, lax.rem(r + d, 8)), device_id_type=MESH)
    for d in range(8):
        pl.semaphore_signal(barrier, inc=1, device_id=(after, lax.rem(r + d, 8)), device_id_type=MESH)
    pl.semaphore_signal(barrier, inc=1, device_id=(before, r), device_id_type=MESH)

    @pl.when(is_relay)
    def _():
        pl.semaphore_signal(barrier, inc=1, device_id=(far, r), device_id_type=MESH)

    @pl.when(is_last)
    def _():
        for z in RELAY_Z:
            pl.semaphore_signal(barrier, inc=1, device_id=(near + 2 * z, r), device_id_type=MESH)

    loads[0].wait()
    for w in range(walkers):
        buf[r, :, w * nocc : (w + 1) * nocc] = orb_own[w]
    targets = 16 + jnp.where(is_relay, 1, 0) + jnp.where(is_source, len(RELAY_Z), 0)
    pl.semaphore_wait(barrier, targets)

    sends = []

    def send(src, dst, send_sem, recv_sem, target):
        copy = pltpu.make_async_remote_copy(
            src_ref=src, dst_ref=dst, send_sem=send_sem, recv_sem=recv_sem,
            device_id=target, device_id_type=MESH,
        )
        copy.start()
        sends.append(copy)
        return copy

    tiles = walkers * nocc // LANE
    pieces = {"A": (0, (tiles + 1) // 2), "B": ((tiles + 1) // 2, tiles // 2)}
    used = [0]

    def pass_on(origin, piece, target):
        i = used[0]
        used[0] += 1
        first, count = pieces[piece]
        ref = buf.at[origin, :, pl.ds(first * LANE, count * LANE)]
        return send(ref, ref, ag_send.at[i], ag_recv.at[i], target)

    up_a, down_b = pass_on(r, "A", up), pass_on(r, "B", down)
    across_a, across_b = pass_on(r, "A", across), pass_on(r, "B", across)
    up_b, down_a = pass_on(r, "B", up), pass_on(r, "A", down)
    green_copy = send(green, green_in, green_sem.at[0], green_sem.at[1], (after, r))

    share = vecs // PARTS

    def fac_copy(i, dst, recv_sem, target):
        return pltpu.make_async_remote_copy(
            src_ref=fac.at[pl.ds(i * share, share)], dst_ref=dst, send_sem=fac_send.at[i], recv_sem=recv_sem,
            device_id=target, device_id_type=MESH,
        )

    def landing(i):
        return fac_in.at[pl.ds(i * share, share)]

    fac_copies = [fac_copy(i, landing(i), fac_recv.at[i], (before, r)) for i in range(PARTS)]

    @pl.when(is_source)
    def _():
        for i, z in enumerate(RELAY_Z, 1):
            fac_copy(i, fac_relay, relay_sem.at[0], (far + 2 * z, r)).start()

    fac_copies[0].start()

    @pl.when(jnp.logical_not(is_source))
    def _():
        for copy in fac_copies[1:]:
            copy.start()

    loads[1].wait()
    loads[2].wait()
    part[0] = partial_bias(green_own, rot_own)
    bias[0, r] = part[0]
    for d in range(1, 8):
        send(part.at[0], bias.at[0, r], bias_send.at[0, d], bias_recv.at[0, r], (l, lax.rem(r + d, 8)))

    up_a.wait_recv()
    pass_2, pass_2x = pass_on(row(0, 3), "A", up), pass_on(row(0, 3), "A", across)
    down_b.wait_recv()
    pass_3, pass_3x = pass_on(row(0, 1), "B", down), pass_on(row(0, 1), "B", across)
    across_a.wait_recv()
    pass_4m = pass_on(row(1, 0), "A", down)
    across_b.wait_recv()
    pass_4p = pass_on(row(1, 0), "B", up)

    def relayed(i):
        return pltpu.make_async_remote_copy(
            src_ref=fac_relay, dst_ref=landing(i), send_sem=relay_sem.at[1], recv_sem=fac_recv.at[i],
            device_id=(near + turn - 1, r), device_id_type=MESH,
        )

    @pl.when(is_relay)
    def _():
        fac_copy(1, fac_relay, relay_sem.at[0], across).wait_recv()

    for i, z in enumerate(RELAY_Z, 1):

        @pl.when(place == 2 * z)
        def _():
            relayed(i).start()

    green_copy.wait_recv()
    part[1] = partial_bias(green_in, rot_own)
    for d in range(8):
        send(part.at[1], bias.at[1, r], bias_send.at[1, d], bias_recv.at[1, r], (before, lax.rem(r + d, 8)))

    block = jnp.int32(0)
    for k in range(peers):
        block = jnp.where(start_pos[k] == l, jnp.int32(k), block)
    table = noise[block]
    columns = table.shape[1]
    row_id = lax.broadcasted_iota(jnp.int32, (columns, 2 * vecs * TILE), 0)
    col_id = lax.broadcasted_iota(jnp.int32, (columns, 2 * vecs * TILE), 1)
    pick = (row_id == lax.rem(l * vecs + col_id // TILE, columns)).astype(F32)
    noise_part = exact_dot(table, pick)

    pass_2x.wait_recv()
    pass_5 = pass_on(row(1, 3), "A", up)
    pass_3x.wait_recv()
    pass_6 = pass_on(row(1, 1), "B", down)

    for s in range(2):
        for d in range(1 - s, 8):
            j = lax.rem(r + d, 8)
            pltpu.make_async_remote_copy(
                src_ref=part.at[s], dst_ref=bias.at[s, j], send_sem=bias_send.at[s, d],
                recv_sem=bias_recv.at[s, j], device_id=across, device_id_type=MESH,
            ).wait_recv()
    sums = []
    for s in range(2):
        total = bias[s, 0]
        for j in range(1, 8):
            total += bias[s, j]
        sums.append(total)
    shifted = (noise_part - jnp.concatenate(sums, axis=1)).astype(BF16).astype(F32)
    depth = 2 * vecs * TILE
    spread = jnp.broadcast_to(shifted[:, None, :], (walkers, TILE, depth)).reshape(walkers * TILE, depth)
    mix[...] = jnp.where(same_slot(walkers * TILE, depth, TILE), spread, 0.0).astype(BF16)
    whole = nrow // TILE
    left = nrow - whole * TILE
    if left:
        row_id = lax.broadcasted_iota(jnp.int32, (depth, 2 * vecs * left), 0)
        col_id = lax.broadcasted_iota(jnp.int32, (depth, 2 * vecs * left), 1)
        few = exact_dot(shifted, (row_id == col_id // left * TILE).astype(F32))
        spread = jnp.broadcast_to(few[:, None, :], (walkers, left, 2 * vecs * left))
        spread = spread.reshape(walkers * left, 2 * vecs * left)
        mix_left[...] = jnp.where(same_slot(walkers * left, 2 * vecs * left, left), spread, 0.0).astype(BF16)

    def operator_of(shard):
        lanes = slice(shard * nrow, (shard + 1) * nrow)

        @pl.loop(0, whole, unroll=whole)
        def _(block):
            rows = pl.ds(pl.multiple_of(block * TILE, TILE), TILE)
            both = jnp.concatenate(
                [f[:, rows, lanes].reshape(vecs * TILE, nrow) for f in (fac_own, fac_in)], axis=0
            )
            result = jnp.dot(mix[...], both, preferred_element_type=F32).astype(BF16)
            oper[shard, :, rows, :] = result.reshape(walkers, TILE, nrow)

        if left:
            rows = slice(whole * TILE, nrow)
            both = jnp.concatenate(
                [f[:, rows, lanes].astype(F32).reshape(vecs * left, nrow) for f in (fac_own, fac_in)], axis=0
            ).astype(BF16)
            result = jnp.dot(mix_left[...], both, preferred_element_type=F32)
            oper[shard, :, rows, :] = result.reshape(walkers, left, nrow).astype(BF16)

    loads[3].wait()
    for copy in fac_copies:
        copy.wait_recv()
    for shard in range(8):
        operator_of(shard)

    def apply(shards, first):
        for w in range(walkers):
            lanes = slice(w * nocc, (w + 1) * nocc)
            total = None if first else out[w]
            for shard in shards:
                product = jnp.dot(oper[shard, w], buf[shard, :, lanes], preferred_element_type=F32)
                total = product if total is None else total + product
            out[w] = total

    for copy in (up_b, down_a, pass_4m, pass_4p):
        copy.wait_recv()
    apply((r, row(0, 1), row(0, 3), row(1, 0)), True)
    for copy in (pass_2, pass_3):
        copy.wait_recv()
    apply((row(0, 2), row(1, 1), row(1, 3)), False)
    for copy in (pass_5, pass_6):
        copy.wait_recv()
    apply((row(1, 2),), False)
    for copy in sends:
        copy.wait_send()
    for copy in fac_copies:
        copy.wait_send()

    @pl.when(is_relay)
    def _():
        relayed(1).wait_send()


def body(start_pos, field_noise, green_half, orbitals, rotated, factors):
    peers = lax.axis_size("loop")
    walkers, nrow, nocc = orbitals.shape
    vecs, _, norb = factors.shape
    width = green_half.shape[2]
    left = nrow % TILE
    dma = pltpu.SemaphoreType.DMA
    vmem, hbm = pl.BlockSpec(memory_space=pltpu.VMEM), pl.BlockSpec(memory_space=pl.ANY)
    return pl.pallas_call(
        functools.partial(kernel, peers),
        out_shape=jax.ShapeDtypeStruct((walkers, nrow, nocc), F32),
        in_specs=[pl.BlockSpec(memory_space=pltpu.SMEM), vmem, hbm, hbm, hbm, hbm],
        out_specs=vmem,
        scratch_shapes=[
            pltpu.VMEM((8, nrow, walkers * nocc), BF16),
            pltpu.VMEM((walkers, nrow, nocc), BF16),
            pltpu.VMEM((walkers, nocc, width), BF16),
            pltpu.VMEM((walkers, nocc, width), BF16),
            pltpu.VMEM((vecs, nocc, width), BF16),
            pltpu.VMEM((vecs, nrow, norb), BF16),
            pltpu.VMEM((vecs, nrow, norb), BF16),
            pltpu.VMEM((vecs // PARTS, nrow, norb), BF16),
            pltpu.VMEM((8, walkers, nrow, nrow), BF16),
            pltpu.VMEM((walkers * TILE, 2 * vecs * TILE), BF16),
            pltpu.VMEM((walkers * left, 2 * vecs * left), BF16),
            pltpu.VMEM((2, walkers, LANE), F32),
            pltpu.VMEM((2, 8, walkers, LANE), F32),
            dma((4,)),
            dma((14,)),
            dma((14,)),
            dma((PARTS,)),
            dma((PARTS,)),
            dma((2,)),
            dma((2,)),
            dma((2, 8)),
            dma((2, 8)),
        ],
        compiler_params=pltpu.CompilerParams(
            collective_id=0, has_side_effects=True, vmem_limit_bytes=60 * 2**20
        ),
        cost_estimate=pl.CostEstimate(
            flops=8 * walkers * nrow * norb * nocc, bytes_accessed=2 * 10**7, transcendentals=0
        ),
    )(start_pos, field_noise, green_half, orbitals, rotated, factors)


def solution(mesh):
    return jax.shard_map(
        body,
        mesh=mesh,
        in_specs=(
            P(),
            P(),
            P("loop", None, "row"),
            P("loop", "row", None),
            P("loop", None, "row"),
            P("loop", "row", None),
        ),
        out_specs=P("loop", "row", None),
        check_vma=False,
    )
```

```python
import functools

import jax
import jax.numpy as jnp
from jax import lax
from jax.experimental import pallas as pl
from jax.experimental.pallas import tpu as pltpu
from jax.sharding import PartitionSpec as P

MESH = pl.DeviceIdType.MESH
F32, BF16 = jnp.float32, jnp.bfloat16
EXACT = lax.Precision.HIGHEST
LANE, TILE = 128, 16
CUTS = (0, 384, 1024, 1600)
ORDER = (0, 1, 2)
ROUND, HERE, MID = 0, 1, 2
LEGS = 4


def same_slot(rows, cols, width):
    row = lax.broadcasted_iota(jnp.int32, (rows, cols), 0)
    col = lax.broadcasted_iota(jnp.int32, (rows, cols), 1)
    return lax.rem(row, width) == lax.rem(col, width)


def group_sum(rows, width):
    row = lax.broadcasted_iota(jnp.int32, (rows, LANE), 0)
    col = lax.broadcasted_iota(jnp.int32, (rows, LANE), 1)
    return (row // width == col // TILE).astype(F32)


def exact_dot(a, b):
    return lax.dot_general(a, b, (((1,), (0,)), ((), ())), precision=EXACT, preferred_element_type=F32)


class Several:
    def __init__(self, whole, parts):
        self.whole, self.parts = whole, parts

    def start(self):
        for part in self.parts:
            part.start()

    def wait_recv(self):
        self.whole().wait_recv()

    def wait_send(self):
        self.whole().wait_send()


def partial_bias(green, rot):
    walkers, nocc, width = green.shape
    vecs = rot.shape[0]
    whole = nocc // TILE
    left = nocc - whole * TILE

    def step(block, total):
        rows = pl.ds(pl.multiple_of(block * TILE, TILE), TILE)
        a = green[:, rows, :].reshape(walkers * TILE, width)
        b = rot[:, rows, :].reshape(vecs * TILE, width)
        return total + lax.dot_general(a, b, (((1,), (1,)), ((), ())), preferred_element_type=F32)

    total = lax.fori_loop(0, whole, step, jnp.zeros((walkers * TILE, vecs * TILE), F32), unroll=True)
    total = jnp.where(same_slot(walkers * TILE, vecs * TILE, TILE), total, 0.0)
    bias = exact_dot(total.reshape(walkers, TILE, vecs * TILE).sum(1), group_sum(vecs * TILE, TILE))
    if left:
        a = green[:, whole * TILE :, :].astype(F32).reshape(walkers * left, width).astype(BF16)
        b = rot[:, whole * TILE :, :].astype(F32).reshape(vecs * left, width).astype(BF16)
        rest = lax.dot_general(a, b, (((1,), (1,)), ((), ())), preferred_element_type=F32)
        rest = jnp.where(same_slot(walkers * left, vecs * left, left), rest, 0.0)
        bias += exact_dot(rest.reshape(walkers, left, vecs * left).sum(1), group_sum(vecs * left, left))
    return bias


def kernel(
    peers, start_pos, noise, green, orb, rot, fac, out,
    buf, orb_own, green_own, rot_own, rot_in, fac_own, fac_in, relay, oper, mix, mix_left, part, bias,
    own_sem, ag_send, ag_recv, fac_send, fac_recv, relay_send, relay_recv, rot_sem, bias_send, bias_recv,
):
    walkers, nrow, nocc = orb_own.shape
    vecs = rot_own.shape[0]
    l, r = lax.axis_index("loop"), lax.axis_index("row")
    half, y = r // 4, lax.rem(r, 4)

    def row(h, step):
        return lax.rem(half + h, 2) * 4 + lax.rem(y + step, 4)

    before, after = lax.rem(l + peers - 1, peers), lax.rem(l + 1, peers)
    up, down, across = (l, row(0, 1)), (l, row(0, 3)), (l, row(1, 0))

    turn = peers // 2
    near, far = (l // turn) * turn, lax.rem((l // turn) * turn + turn, peers)
    place = lax.rem(l, turn)
    mid, last = turn // 2, turn - 2
    is_source, is_mid, is_round, is_last = [place == at for at in (0, mid, last, turn - 1)]

    loads = [
        pltpu.make_async_copy(src, dst, own_sem.at[i])
        for i, (src, dst) in enumerate(
            ((orb, orb_own), (green, green_own), (rot, rot_own), (fac, fac_own))
        )
    ]
    for load in loads:
        load.start()

    barrier = pltpu.get_barrier_semaphore()
    for d in range(1, 8):
        pl.semaphore_signal(barrier, inc=1, device_id=(l, lax.rem(r + d, 8)), device_id_type=MESH)
    pl.semaphore_signal(barrier, inc=1, device_id=(after, r), device_id_type=MESH)

    def greet(position):
        pl.semaphore_signal(barrier, inc=1, device_id=(position, r), device_id_type=MESH)

    @pl.when(is_source | is_mid)
    def _():
        greet(far)

    @pl.when(is_round)
    def _():
        greet(near)

    @pl.when(is_last)
    def _():
        greet(near)
        greet(near + mid)
        greet(far + last)

    loads[0].wait()
    for w in range(walkers):
        buf[r, :, w * nocc : (w + 1) * nocc] = orb_own[w]
    targets = 8 + jnp.where(is_source, 4, 0) + jnp.where(is_mid | is_round, 1, 0)
    pl.semaphore_wait(barrier, targets)

    sends = []

    def send(src, dst, send_sem, recv_sem, target):
        copy = pltpu.make_async_remote_copy(
            src_ref=src, dst_ref=dst, send_sem=send_sem, recv_sem=recv_sem,
            device_id=target, device_id_type=MESH,
        )
        copy.start()
        sends.append(copy)
        return copy

    tiles = walkers * nocc // LANE
    top = (tiles + 1) // 2
    pieces = {"A": (0, top), "B": (top, tiles - top)}
    used = [0]

    def pass_on(origin, piece, target):
        i = used[0]
        used[0] += 1
        first, count = pieces[piece]
        ref = buf.at[origin, :, pl.ds(first * LANE, count * LANE)]
        return send(ref, ref, ag_send.at[i], ag_recv.at[i], target)

    def cut(i):
        return pl.ds(CUTS[i], CUTS[i + 1] - CUTS[i])

    def fac_copy(i, src, dst, send_sem, recv_sem, target):
        return pltpu.make_async_remote_copy(
            src_ref=src, dst_ref=dst, send_sem=send_sem, recv_sem=recv_sem,
            device_id=(target, r), device_id_type=MESH,
        )

    def vectors(first, count, i, ref):
        return ref.at[pl.ds(first, count), :, cut(i)]

    def several(i, src, dst, send_sem, recv_sems, target):
        def some(first, count, recv_sem):
            return fac_copy(
                i, vectors(first, count, i, src), vectors(first, count, i, dst), send_sem, recv_sem, target
            )

        step = vecs // len(recv_sems)
        whole = functools.partial(some, 0, vecs, recv_sems[0])
        return Several(whole, [some(k * step, step, sem) for k, sem in enumerate(recv_sems)])

    def direct(i):
        return several(i, fac, fac_in, fac_send.at[i], [fac_recv.at[i]], before)

    def first_leg(i, target):
        return several(i, fac, relay, fac_send.at[i], [relay_recv.at[k] for k in range(LEGS)], target)

    def last_leg(i, target):
        return several(i, relay, fac_in, relay_send.at[0], [fac_recv.at[i]] * LEGS, target)

    def hand_over(first, last):
        for here, there in zip(first.parts, last.parts):
            here.wait_recv()
            there.start()

    fac_copies = [direct(i) for i in range(len(CUTS) - 1)]
    to_here, from_here = first_leg(HERE, far), last_leg(HERE, near + turn - 1)
    to_round, from_round = first_leg(ROUND, near + last), last_leg(ROUND, far + turn - 1)
    to_mid, from_mid = first_leg(MID, far + mid), last_leg(MID, near + turn - 1)

    rot_copy = send(rot, rot_in, rot_sem.at[0], rot_sem.at[1], (before, r))
    across_a, across_b = pass_on(r, "A", across), pass_on(r, "B", across)
    up_a, down_b = pass_on(r, "A", up), pass_on(r, "B", down)
    up_b, down_a = pass_on(r, "B", up), pass_on(r, "A", down)
    @pl.when(is_source)
    def _():
        to_round.start()
        to_mid.start()

    @pl.when(jnp.logical_not(is_source))
    def _():
        for i in ORDER:
            fac_copies[i].start()

    loads[1].wait()
    loads[2].wait()
    part[0] = partial_bias(green_own, rot_own)
    bias[0, r] = part[0]
    for d in range(1, 8):
        send(part.at[0], bias.at[0, r], bias_send.at[0, d], bias_recv.at[0, r], (l, lax.rem(r + d, 8)))

    rot_copy.wait_recv()
    part[1] = partial_bias(green_own, rot_in)
    bias[1, r] = part[1]
    for d in range(1, 8):
        send(part.at[1], bias.at[1, r], bias_send.at[1, d], bias_recv.at[1, r], (l, lax.rem(r + d, 8)))
    out[...] = jnp.zeros_like(out)

    up_a.wait_recv()
    pass_2 = pass_on(row(0, 3), "A", up)
    down_b.wait_recv()
    pass_3 = pass_on(row(0, 1), "B", down)
    @pl.when(is_source)
    def _():
        to_here.start()

    @pl.when(is_round)
    def _():
        hand_over(to_round, from_round)

    across_b.wait_recv()
    pass_4p = pass_on(row(1, 0), "B", up)
    across_a.wait_recv()
    pass_4m = pass_on(row(1, 0), "A", down)

    pass_2x, pass_3x = pass_on(row(0, 3), "A", across), pass_on(row(0, 1), "B", across)

    @pl.when(is_source)
    def _():
        hand_over(to_here, from_here)

    @pl.when(is_mid)
    def _():
        hand_over(to_mid, from_mid)

    block = jnp.int32(0)
    for k in range(peers):
        block = jnp.where(start_pos[k] == l, jnp.int32(k), block)
    table = noise[block]
    columns = table.shape[1]
    row_id = lax.broadcasted_iota(jnp.int32, (columns, 2 * vecs * TILE), 0)
    col_id = lax.broadcasted_iota(jnp.int32, (columns, 2 * vecs * TILE), 1)
    pick = (row_id == lax.rem(l * vecs + col_id // TILE, columns)).astype(F32)
    noise_part = exact_dot(table, pick)

    pass_4p.wait_recv()
    pass_5 = pass_on(row(1, 3), "B", up)
    pass_4m.wait_recv()
    pass_6 = pass_on(row(1, 1), "A", down)
    for s in range(2):
        for d in range(1, 8):
            j = lax.rem(r + d, 8)
            pltpu.make_async_remote_copy(
                src_ref=part.at[s], dst_ref=bias.at[s, j], send_sem=bias_send.at[s, d],
                recv_sem=bias_recv.at[s, j], device_id=across, device_id_type=MESH,
            ).wait_recv()
    sums = []
    for s in range(2):
        total = bias[s, 0]
        for j in range(1, 8):
            total += bias[s, j]
        sums.append(total)
    shifted = (noise_part - jnp.concatenate(sums, axis=1)).astype(BF16).astype(F32)
    depth = 2 * vecs * TILE
    spread = jnp.broadcast_to(shifted[:, None, :], (walkers, TILE, depth)).reshape(walkers * TILE, depth)
    mix[...] = jnp.where(same_slot(walkers * TILE, depth, TILE), spread, 0.0).astype(BF16)
    whole = nrow // TILE
    left = nrow - whole * TILE
    if left:
        row_id = lax.broadcasted_iota(jnp.int32, (depth, 2 * vecs * left), 0)
        col_id = lax.broadcasted_iota(jnp.int32, (depth, 2 * vecs * left), 1)
        few = exact_dot(shifted, (row_id == col_id // left * TILE).astype(F32))
        spread = jnp.broadcast_to(few[:, None, :], (walkers, left, 2 * vecs * left))
        spread = spread.reshape(walkers * left, 2 * vecs * left)
        mix_left[...] = jnp.where(same_slot(walkers * left, 2 * vecs * left, left), spread, 0.0).astype(BF16)

    def operator_of(shard):
        lanes = slice(shard * nrow, (shard + 1) * nrow)

        @pl.loop(0, whole, unroll=whole)
        def _(block):
            rows = pl.ds(pl.multiple_of(block * TILE, TILE), TILE)
            both = jnp.concatenate(
                [f[:, rows, lanes].reshape(vecs * TILE, nrow) for f in (fac_own, fac_in)], axis=0
            )
            result = jnp.dot(mix[...], both, preferred_element_type=F32).astype(BF16)
            oper[shard, :, rows, :] = result.reshape(walkers, TILE, nrow)

        if left:
            rows = slice(whole * TILE, nrow)
            both = jnp.concatenate(
                [f[:, rows, lanes].astype(F32).reshape(vecs * left, nrow) for f in (fac_own, fac_in)], axis=0
            ).astype(BF16)
            result = jnp.dot(mix_left[...], both, preferred_element_type=F32)
            oper[shard, :, rows, :] = result.reshape(walkers, left, nrow).astype(BF16)

    def apply(shards):
        for w in range(walkers):
            lanes = slice(w * nocc, (w + 1) * nocc)
            total = out[w]
            for shard in shards:
                total += jnp.dot(oper[shard, w], buf[shard, :, lanes], preferred_element_type=F32)
            out[w] = total

    for copy in (up_b, down_a):
        copy.wait_recv()
    loads[3].wait()
    seen = [False] * len(ORDER)
    done = set()
    for i in ORDER:
        fac_copies[i].wait_recv()
        seen[i] = True
        ready = []
        for shard in range(8):
            parts = [k for k in range(len(ORDER)) if CUTS[k] < (shard + 1) * nrow and CUTS[k + 1] > shard * nrow]
            if shard not in done and all(seen[k] for k in parts):
                ready.append(shard)
                operator_of(shard)
        done.update(ready)

        @pl.loop(ready[0], ready[-1] + 1)
        def _(shard):
            along = lax.rem(shard % 4 - y + 4, 4)
            early = jnp.where(shard // 4 == half, along != 2, along == 0)

            @pl.when(early)
            def _():
                apply((shard,))

    for copy in (pass_2x, pass_3x, pass_2, pass_3):
        copy.wait_recv()
    apply((row(0, 2), row(1, 1), row(1, 3)))
    for copy in (pass_5, pass_6):
        copy.wait_recv()
    apply((row(1, 2),))
    for copy in sends:
        copy.wait_send()
    for copy in fac_copies:
        copy.wait_send()

    @pl.when(is_source)
    def _():
        from_here.wait_send()

    @pl.when(is_round)
    def _():
        from_round.wait_send()

    @pl.when(is_mid)
    def _():
        from_mid.wait_send()


def body(start_pos, field_noise, green_half, orbitals, rotated, factors):
    peers = lax.axis_size("loop")
    walkers, nrow, nocc = orbitals.shape
    vecs, _, norb = factors.shape
    width = green_half.shape[2]
    left = nrow % TILE
    dma = pltpu.SemaphoreType.DMA
    vmem, hbm = pl.BlockSpec(memory_space=pltpu.VMEM), pl.BlockSpec(memory_space=pl.ANY)
    return pl.pallas_call(
        functools.partial(kernel, peers),
        out_shape=jax.ShapeDtypeStruct((walkers, nrow, nocc), F32),
        in_specs=[pl.BlockSpec(memory_space=pltpu.SMEM), vmem, hbm, hbm, hbm, hbm],
        out_specs=vmem,
        scratch_shapes=[
            pltpu.VMEM((8, nrow, walkers * nocc), BF16),
            pltpu.VMEM((walkers, nrow, nocc), BF16),
            pltpu.VMEM((walkers, nocc, width), BF16),
            pltpu.VMEM((vecs, nocc, width), BF16),
            pltpu.VMEM((vecs, nocc, width), BF16),
            pltpu.VMEM((vecs, nrow, norb), BF16),
            pltpu.VMEM((vecs, nrow, norb), BF16),
            pltpu.VMEM((vecs, nrow, norb), BF16),
            pltpu.VMEM((8, walkers, nrow, nrow), BF16),
            pltpu.VMEM((walkers * TILE, 2 * vecs * TILE), BF16),
            pltpu.VMEM((walkers * left, 2 * vecs * left), BF16),
            pltpu.VMEM((2, walkers, LANE), F32),
            pltpu.VMEM((2, 8, walkers, LANE), F32),
            dma((4,)),
            dma((14,)),
            dma((14,)),
            dma((len(ORDER),)),
            dma((len(ORDER),)),
            dma((1,)),
            dma((LEGS,)),
            dma((2,)),
            dma((2, 8)),
            dma((2, 8)),
        ],
        compiler_params=pltpu.CompilerParams(
            collective_id=0, has_side_effects=True, vmem_limit_bytes=60 * 2**20
        ),
        cost_estimate=pl.CostEstimate(
            flops=8 * walkers * nrow * norb * nocc, bytes_accessed=2 * 10**7, transcendentals=0
        ),
    )(start_pos, field_noise, green_half, orbitals, rotated, factors)


def solution(mesh):
    return jax.shard_map(
        body,
        mesh=mesh,
        in_specs=(
            P(),
            P(),
            P("loop", None, "row"),
            P("loop", "row", None),
            P("loop", None, "row"),
            P("loop", "row", None),
        ),
        out_specs=P("loop", "row", None),
        check_vma=False,
    )
```

```python
import functools

import jax
import jax.numpy as jnp
from jax import lax
from jax.experimental import pallas as pl
from jax.experimental.pallas import tpu as pltpu
from jax.sharding import PartitionSpec as P

MESH = pl.DeviceIdType.MESH
F32, BF16 = jnp.float32, jnp.bfloat16
EXACT = lax.Precision.HIGHEST
LANE, TILE = 128, 16
CUTS = (0, 256, 640, 1152, 1600)
ORDER = (0, 2, 3, 1)
ROUND, LATE, HERE, MID = 0, 1, 2, 3
LEGS = 4


def same_slot(rows, cols, width):
    row = lax.broadcasted_iota(jnp.int32, (rows, cols), 0)
    col = lax.broadcasted_iota(jnp.int32, (rows, cols), 1)
    return lax.rem(row, width) == lax.rem(col, width)


def group_sum(rows, width):
    row = lax.broadcasted_iota(jnp.int32, (rows, LANE), 0)
    col = lax.broadcasted_iota(jnp.int32, (rows, LANE), 1)
    return (row // width == col // TILE).astype(F32)


def exact_dot(a, b):
    return lax.dot_general(a, b, (((1,), (0,)), ((), ())), precision=EXACT, preferred_element_type=F32)


class Several:
    def __init__(self, whole, parts):
        self.whole, self.parts = whole, parts

    def start(self):
        for part in self.parts:
            part.start()

    def wait_recv(self):
        self.whole().wait_recv()

    def wait_send(self):
        self.whole().wait_send()


def partial_bias(green, rot):
    walkers, nocc, width = green.shape
    vecs = rot.shape[0]
    whole = nocc // TILE
    left = nocc - whole * TILE

    def step(block, total):
        rows = pl.ds(pl.multiple_of(block * TILE, TILE), TILE)
        a = green[:, rows, :].reshape(walkers * TILE, width)
        b = rot[:, rows, :].reshape(vecs * TILE, width)
        return total + lax.dot_general(a, b, (((1,), (1,)), ((), ())), preferred_element_type=F32)

    total = lax.fori_loop(0, whole, step, jnp.zeros((walkers * TILE, vecs * TILE), F32), unroll=True)
    total = jnp.where(same_slot(walkers * TILE, vecs * TILE, TILE), total, 0.0)
    bias = exact_dot(total.reshape(walkers, TILE, vecs * TILE).sum(1), group_sum(vecs * TILE, TILE))
    if left:
        a = green[:, whole * TILE :, :].astype(F32).reshape(walkers * left, width).astype(BF16)
        b = rot[:, whole * TILE :, :].astype(F32).reshape(vecs * left, width).astype(BF16)
        rest = lax.dot_general(a, b, (((1,), (1,)), ((), ())), preferred_element_type=F32)
        rest = jnp.where(same_slot(walkers * left, vecs * left, left), rest, 0.0)
        bias += exact_dot(rest.reshape(walkers, left, vecs * left).sum(1), group_sum(vecs * left, left))
    return bias


def kernel(
    peers, start_pos, noise, green, orb, rot, fac, out,
    buf, orb_own, green_own, rot_own, rot_in, fac_own, fac_in, relay, oper, mix, mix_left, part, bias,
    own_sem, ag_send, ag_recv, fac_send, fac_recv, relay_send, relay_recv, rot_sem, bias_send, bias_recv,
):
    walkers, nrow, nocc = orb_own.shape
    vecs = rot_own.shape[0]
    l, r = lax.axis_index("loop"), lax.axis_index("row")
    half, y = r // 4, lax.rem(r, 4)

    def row(h, step):
        return lax.rem(half + h, 2) * 4 + lax.rem(y + step, 4)

    before, after = lax.rem(l + peers - 1, peers), lax.rem(l + 1, peers)
    up, down, across = (l, row(0, 1)), (l, row(0, 3)), (l, row(1, 0))

    turn = peers // 2
    near, far = (l // turn) * turn, lax.rem((l // turn) * turn + turn, peers)
    place = lax.rem(l, turn)
    hop, mid, late, last = turn // 4, turn // 2, turn - 4, turn - 2
    is_source, is_hop, is_mid, is_late, is_round, is_last = [
        place == at for at in (0, hop, mid, late, last, turn - 1)
    ]

    loads = [
        pltpu.make_async_copy(src, dst, own_sem.at[i])
        for i, (src, dst) in enumerate(
            ((orb, orb_own), (green, green_own), (rot, rot_own), (fac, fac_own))
        )
    ]
    for load in loads:
        load.start()

    barrier = pltpu.get_barrier_semaphore()
    for d in range(1, 8):
        pl.semaphore_signal(barrier, inc=1, device_id=(l, lax.rem(r + d, 8)), device_id_type=MESH)
    pl.semaphore_signal(barrier, inc=1, device_id=(after, r), device_id_type=MESH)

    def greet(position):
        pl.semaphore_signal(barrier, inc=1, device_id=(position, r), device_id_type=MESH)

    @pl.when(is_source | is_mid)
    def _():
        greet(far)

    @pl.when(is_round | is_hop)
    def _():
        greet(near)

    @pl.when(is_late)
    def _():
        greet(far + hop)

    @pl.when(is_last)
    def _():
        greet(near)
        greet(near + mid)
        greet(near + late)
        greet(far + last)

    loads[0].wait()
    for w in range(walkers):
        buf[r, :, w * nocc : (w + 1) * nocc] = orb_own[w]
    targets = 8 + jnp.where(is_source, 5, 0) + jnp.where(is_hop | is_mid | is_late | is_round, 1, 0)
    pl.semaphore_wait(barrier, targets)

    sends = []

    def send(src, dst, send_sem, recv_sem, target):
        copy = pltpu.make_async_remote_copy(
            src_ref=src, dst_ref=dst, send_sem=send_sem, recv_sem=recv_sem,
            device_id=target, device_id_type=MESH,
        )
        copy.start()
        sends.append(copy)
        return copy

    tiles = walkers * nocc // LANE
    top = (tiles + 1) // 2
    mid_a, mid_b = (top + 1) // 2, (top + tiles) // 2
    pieces = {
        "A": (0, top), "A1": (0, mid_a), "A2": (mid_a, top - mid_a),
        "B": (top, tiles - top), "B1": (top, mid_b - top), "B2": (mid_b, tiles - mid_b),
    }
    used = [0]

    def pass_on(origin, piece, target):
        i = used[0]
        used[0] += 1
        first, count = pieces[piece]
        ref = buf.at[origin, :, pl.ds(first * LANE, count * LANE)]
        return send(ref, ref, ag_send.at[i], ag_recv.at[i], target)

    def cut(i):
        return pl.ds(CUTS[i], CUTS[i + 1] - CUTS[i])

    def fac_copy(i, src, dst, send_sem, recv_sem, target):
        return pltpu.make_async_remote_copy(
            src_ref=src, dst_ref=dst, send_sem=send_sem, recv_sem=recv_sem,
            device_id=(target, r), device_id_type=MESH,
        )

    def vectors(first, count, i, ref):
        return ref.at[pl.ds(first, count), :, cut(i)]

    def several(i, src, dst, send_sem, recv_sems, target):
        def some(first, count, recv_sem):
            return fac_copy(
                i, vectors(first, count, i, src), vectors(first, count, i, dst), send_sem, recv_sem, target
            )

        step = vecs // len(recv_sems)
        whole = functools.partial(some, 0, vecs, recv_sems[0])
        return Several(whole, [some(k * step, step, sem) for k, sem in enumerate(recv_sems)])

    def direct(i):
        return several(i, fac, fac_in, fac_send.at[i], [fac_recv.at[i]], before)

    def first_leg(i, target):
        return several(i, fac, relay, fac_send.at[i], [relay_recv.at[k] for k in range(LEGS)], target)

    def last_leg(i, target):
        return several(i, relay, fac_in, relay_send.at[0], [fac_recv.at[i]] * LEGS, target)

    def next_leg(i, target):
        return several(i, relay, relay, relay_send.at[0], [relay_recv.at[k] for k in range(LEGS)], target)

    def hand_over(first, last):
        for here, there in zip(first.parts, last.parts):
            here.wait_recv()
            there.start()

    fac_copies = [direct(i) for i in range(len(CUTS) - 1)]
    to_here, from_here = first_leg(HERE, far), last_leg(HERE, near + turn - 1)
    to_round, from_round = first_leg(ROUND, near + last), last_leg(ROUND, far + turn - 1)
    to_hop, to_late, from_late = first_leg(LATE, near + hop), next_leg(LATE, far + late), last_leg(LATE, near + turn - 1)
    to_mid, from_mid = first_leg(MID, far + mid), last_leg(MID, near + turn - 1)

    rot_copy = send(rot, rot_in, rot_sem.at[0], rot_sem.at[1], (before, r))
    across_a, across_b = pass_on(r, "A", across), pass_on(r, "B", across)
    up_a, down_b = pass_on(r, "A", up), pass_on(r, "B", down)
    up_b, down_a = pass_on(r, "B", up), pass_on(r, "A", down)
    @pl.when(is_source)
    def _():
        to_round.start()
        to_hop.start()
        to_mid.start()

    def send_parts(*parts):
        @pl.when(jnp.logical_not(is_source))
        def _():
            for i in parts:
                fac_copies[i].start()

    send_parts(*ORDER[:2])

    loads[1].wait()
    loads[2].wait()
    part[0] = partial_bias(green_own, rot_own)
    bias[0, r] = part[0]
    for d in range(1, 8):
        send(part.at[0], bias.at[0, r], bias_send.at[0, d], bias_recv.at[0, r], (l, lax.rem(r + d, 8)))

    rot_copy.wait_recv()
    part[1] = partial_bias(green_own, rot_in)
    bias[1, r] = part[1]
    for d in range(1, 8):
        send(part.at[1], bias.at[1, r], bias_send.at[1, d], bias_recv.at[1, r], (l, lax.rem(r + d, 8)))
    out[...] = jnp.zeros_like(out)

    up_a.wait_recv()
    pass_2 = pass_on(row(0, 3), "A", up)
    down_b.wait_recv()
    pass_3 = pass_on(row(0, 1), "B", down)
    send_parts(ORDER[2])
    @pl.when(is_source)
    def _():
        to_here.start()

    @pl.when(is_round)
    def _():
        hand_over(to_round, from_round)

    @pl.when(is_hop)
    def _():
        hand_over(to_hop, to_late)

    across_b.wait_recv()
    pass_4p = pass_on(row(1, 0), "B1", up), pass_on(row(1, 0), "B2", up)
    across_a.wait_recv()
    pass_4m = pass_on(row(1, 0), "A1", down), pass_on(row(1, 0), "A2", down)

    send_parts(ORDER[3])
    pass_2x, pass_3x = pass_on(row(0, 3), "A", across), pass_on(row(0, 1), "B", across)

    @pl.when(is_source)
    def _():
        hand_over(to_here, from_here)

    @pl.when(is_mid)
    def _():
        hand_over(to_mid, from_mid)

    @pl.when(is_late)
    def _():
        hand_over(to_late, from_late)

    block = jnp.int32(0)
    for k in range(peers):
        block = jnp.where(start_pos[k] == l, jnp.int32(k), block)
    table = noise[block]
    columns = table.shape[1]
    row_id = lax.broadcasted_iota(jnp.int32, (columns, 2 * vecs * TILE), 0)
    col_id = lax.broadcasted_iota(jnp.int32, (columns, 2 * vecs * TILE), 1)
    pick = (row_id == lax.rem(l * vecs + col_id // TILE, columns)).astype(F32)
    noise_part = exact_dot(table, pick)

    final = []
    for i in range(2):
        pass_4p[i].wait_recv()
        final.append(pass_on(row(1, 3), ("B1", "B2")[i], up))
        pass_4m[i].wait_recv()
        final.append(pass_on(row(1, 1), ("A1", "A2")[i], down))

    for s in range(2):
        for d in range(1, 8):
            j = lax.rem(r + d, 8)
            pltpu.make_async_remote_copy(
                src_ref=part.at[s], dst_ref=bias.at[s, j], send_sem=bias_send.at[s, d],
                recv_sem=bias_recv.at[s, j], device_id=across, device_id_type=MESH,
            ).wait_recv()
    sums = []
    for s in range(2):
        total = bias[s, 0]
        for j in range(1, 8):
            total += bias[s, j]
        sums.append(total)
    shifted = (noise_part - jnp.concatenate(sums, axis=1)).astype(BF16).astype(F32)
    depth = 2 * vecs * TILE
    spread = jnp.broadcast_to(shifted[:, None, :], (walkers, TILE, depth)).reshape(walkers * TILE, depth)
    mix[...] = jnp.where(same_slot(walkers * TILE, depth, TILE), spread, 0.0).astype(BF16)
    whole = nrow // TILE
    left = nrow - whole * TILE
    if left:
        row_id = lax.broadcasted_iota(jnp.int32, (depth, 2 * vecs * left), 0)
        col_id = lax.broadcasted_iota(jnp.int32, (depth, 2 * vecs * left), 1)
        few = exact_dot(shifted, (row_id == col_id // left * TILE).astype(F32))
        spread = jnp.broadcast_to(few[:, None, :], (walkers, left, 2 * vecs * left))
        spread = spread.reshape(walkers * left, 2 * vecs * left)
        mix_left[...] = jnp.where(same_slot(walkers * left, 2 * vecs * left, left), spread, 0.0).astype(BF16)

    def operator_of(shard):
        lanes = slice(shard * nrow, (shard + 1) * nrow)

        @pl.loop(0, whole, unroll=whole)
        def _(block):
            rows = pl.ds(pl.multiple_of(block * TILE, TILE), TILE)
            both = jnp.concatenate(
                [f[:, rows, lanes].reshape(vecs * TILE, nrow) for f in (fac_own, fac_in)], axis=0
            )
            result = jnp.dot(mix[...], both, preferred_element_type=F32).astype(BF16)
            oper[shard, :, rows, :] = result.reshape(walkers, TILE, nrow)

        if left:
            rows = slice(whole * TILE, nrow)
            both = jnp.concatenate(
                [f[:, rows, lanes].astype(F32).reshape(vecs * left, nrow) for f in (fac_own, fac_in)], axis=0
            ).astype(BF16)
            result = jnp.dot(mix_left[...], both, preferred_element_type=F32)
            oper[shard, :, rows, :] = result.reshape(walkers, left, nrow).astype(BF16)

    def apply(shards):
        for w in range(walkers):
            lanes = slice(w * nocc, (w + 1) * nocc)
            total = out[w]
            for shard in shards:
                total += jnp.dot(oper[shard, w], buf[shard, :, lanes], preferred_element_type=F32)
            out[w] = total

    for copy in (up_b, down_a):
        copy.wait_recv()
    loads[3].wait()
    seen = [False] * len(ORDER)
    done = set()
    for i in ORDER:
        fac_copies[i].wait_recv()
        seen[i] = True
        ready = []
        for shard in range(8):
            parts = [k for k in range(len(ORDER)) if CUTS[k] < (shard + 1) * nrow and CUTS[k + 1] > shard * nrow]
            if shard not in done and all(seen[k] for k in parts):
                ready.append(shard)
                operator_of(shard)
        done.update(ready)

        @pl.loop(ready[0], ready[-1] + 1)
        def _(shard):
            along = lax.rem(shard % 4 - y + 4, 4)
            early = jnp.where(shard // 4 == half, along != 2, along == 0)

            @pl.when(early)
            def _():
                apply((shard,))

    for copy in (pass_2x, pass_3x, pass_2, pass_3):
        copy.wait_recv()
    apply((row(0, 2), row(1, 1), row(1, 3)))
    for copy in final:
        copy.wait_recv()
    apply((row(1, 2),))
    for copy in sends:
        copy.wait_send()
    for copy in fac_copies:
        copy.wait_send()

    @pl.when(is_source)
    def _():
        from_here.wait_send()

    @pl.when(is_round)
    def _():
        from_round.wait_send()

    @pl.when(is_hop)
    def _():
        to_late.wait_send()

    @pl.when(is_late)
    def _():
        from_late.wait_send()

    @pl.when(is_mid)
    def _():
        from_mid.wait_send()


def body(start_pos, field_noise, green_half, orbitals, rotated, factors):
    peers = lax.axis_size("loop")
    walkers, nrow, nocc = orbitals.shape
    vecs, _, norb = factors.shape
    width = green_half.shape[2]
    left = nrow % TILE
    dma = pltpu.SemaphoreType.DMA
    vmem, hbm = pl.BlockSpec(memory_space=pltpu.VMEM), pl.BlockSpec(memory_space=pl.ANY)
    return pl.pallas_call(
        functools.partial(kernel, peers),
        out_shape=jax.ShapeDtypeStruct((walkers, nrow, nocc), F32),
        in_specs=[pl.BlockSpec(memory_space=pltpu.SMEM), vmem, hbm, hbm, hbm, hbm],
        out_specs=vmem,
        scratch_shapes=[
            pltpu.VMEM((8, nrow, walkers * nocc), BF16),
            pltpu.VMEM((walkers, nrow, nocc), BF16),
            pltpu.VMEM((walkers, nocc, width), BF16),
            pltpu.VMEM((vecs, nocc, width), BF16),
            pltpu.VMEM((vecs, nocc, width), BF16),
            pltpu.VMEM((vecs, nrow, norb), BF16),
            pltpu.VMEM((vecs, nrow, norb), BF16),
            pltpu.VMEM((vecs, nrow, norb), BF16),
            pltpu.VMEM((8, walkers, nrow, nrow), BF16),
            pltpu.VMEM((walkers * TILE, 2 * vecs * TILE), BF16),
            pltpu.VMEM((walkers * left, 2 * vecs * left), BF16),
            pltpu.VMEM((2, walkers, LANE), F32),
            pltpu.VMEM((2, 8, walkers, LANE), F32),
            dma((4,)),
            dma((18,)),
            dma((18,)),
            dma((len(ORDER),)),
            dma((len(ORDER),)),
            dma((1,)),
            dma((LEGS,)),
            dma((2,)),
            dma((2, 8)),
            dma((2, 8)),
        ],
        compiler_params=pltpu.CompilerParams(
            collective_id=0, has_side_effects=True, vmem_limit_bytes=60 * 2**20
        ),
        cost_estimate=pl.CostEstimate(
            flops=8 * walkers * nrow * norb * nocc, bytes_accessed=2 * 10**7, transcendentals=0
        ),
    )(start_pos, field_noise, green_half, orbitals, rotated, factors)


def solution(mesh):
    return jax.shard_map(
        body,
        mesh=mesh,
        in_specs=(
            P(),
            P(),
            P("loop", None, "row"),
            P("loop", "row", None),
            P("loop", None, "row"),
            P("loop", "row", None),
        ),
        out_specs=P("loop", "row", None),
        check_vma=False,
    )
```

```python
import functools

import jax
import jax.numpy as jnp
from jax import lax
from jax.experimental import pallas as pl
from jax.experimental.pallas import tpu as pltpu
from jax.sharding import PartitionSpec as P

MESH = pl.DeviceIdType.MESH
F32, BF16 = jnp.float32, jnp.bfloat16
EXACT = lax.Precision.HIGHEST
LANE, TILE = 128, 16
CUTS = (0, 256, 640, 1152, 1600)
ORDER = (0, 2, 3, 1)
ROUND, LATE, HERE, MID = 0, 1, 2, 3
LEGS = 4


def same_slot(rows, cols, width):
    row = lax.broadcasted_iota(jnp.int32, (rows, cols), 0)
    col = lax.broadcasted_iota(jnp.int32, (rows, cols), 1)
    return lax.rem(row, width) == lax.rem(col, width)


def group_sum(rows, width):
    row = lax.broadcasted_iota(jnp.int32, (rows, LANE), 0)
    col = lax.broadcasted_iota(jnp.int32, (rows, LANE), 1)
    return (row // width == col // TILE).astype(F32)


def exact_dot(a, b):
    return lax.dot_general(a, b, (((1,), (0,)), ((), ())), precision=EXACT, preferred_element_type=F32)


class Several:
    def __init__(self, whole, parts):
        self.whole, self.parts = whole, parts

    def start(self):
        for part in self.parts:
            part.start()

    def wait_recv(self):
        self.whole().wait_recv()

    def wait_send(self):
        self.whole().wait_send()


def partial_bias(green, rot):
    walkers, nocc, width = green.shape
    vecs = rot.shape[0]
    whole = nocc // TILE
    left = nocc - whole * TILE

    def step(block, total):
        rows = pl.ds(pl.multiple_of(block * TILE, TILE), TILE)
        a = green[:, rows, :].reshape(walkers * TILE, width)
        b = rot[:, rows, :].reshape(vecs * TILE, width)
        return total + lax.dot_general(a, b, (((1,), (1,)), ((), ())), preferred_element_type=F32)

    total = lax.fori_loop(0, whole, step, jnp.zeros((walkers * TILE, vecs * TILE), F32), unroll=True)
    total = jnp.where(same_slot(walkers * TILE, vecs * TILE, TILE), total, 0.0)
    bias = exact_dot(total.reshape(walkers, TILE, vecs * TILE).sum(1), group_sum(vecs * TILE, TILE))
    if left:
        a = green[:, whole * TILE :, :].astype(F32).reshape(walkers * left, width).astype(BF16)
        b = rot[:, whole * TILE :, :].astype(F32).reshape(vecs * left, width).astype(BF16)
        rest = lax.dot_general(a, b, (((1,), (1,)), ((), ())), preferred_element_type=F32)
        rest = jnp.where(same_slot(walkers * left, vecs * left, left), rest, 0.0)
        bias += exact_dot(rest.reshape(walkers, left, vecs * left).sum(1), group_sum(vecs * left, left))
    return bias


def kernel(
    peers, start_pos, noise, green, orb, rot, fac, out,
    buf, orb_own, green_own, rot_own, rot_in, fac_own, fac_in, relay, oper, mix, mix_left, part, bias,
    own_sem, ag_send, ag_recv, fac_send, fac_recv, relay_send, relay_recv, rot_sem, bias_send, bias_recv,
):
    walkers, nrow, nocc = orb_own.shape
    vecs = rot_own.shape[0]
    l, r = lax.axis_index("loop"), lax.axis_index("row")
    half, y = r // 4, lax.rem(r, 4)

    def row(h, step):
        return lax.rem(half + h, 2) * 4 + lax.rem(y + step, 4)

    before, after = lax.rem(l + peers - 1, peers), lax.rem(l + 1, peers)
    up, down, across = (l, row(0, 1)), (l, row(0, 3)), (l, row(1, 0))

    turn = peers // 2
    near, far = (l // turn) * turn, lax.rem((l // turn) * turn + turn, peers)
    place = lax.rem(l, turn)
    hop, mid, late, last = turn // 4, turn // 2, turn - 4, turn - 2
    is_source, is_hop, is_mid, is_late, is_round, is_last = [
        place == at for at in (0, hop, mid, late, last, turn - 1)
    ]

    loads = [
        pltpu.make_async_copy(src, dst, own_sem.at[i])
        for i, (src, dst) in enumerate(
            ((orb, orb_own), (green, green_own), (rot, rot_own), (fac, fac_own))
        )
    ]
    for load in loads:
        load.start()

    barrier = pltpu.get_barrier_semaphore()
    for d in range(1, 8):
        pl.semaphore_signal(barrier, inc=1, device_id=(l, lax.rem(r + d, 8)), device_id_type=MESH)
    pl.semaphore_signal(barrier, inc=1, device_id=(after, r), device_id_type=MESH)

    def greet(position):
        pl.semaphore_signal(barrier, inc=1, device_id=(position, r), device_id_type=MESH)

    @pl.when(is_source | is_mid)
    def _():
        greet(far)

    @pl.when(is_round | is_hop)
    def _():
        greet(near)

    @pl.when(is_late)
    def _():
        greet(far + hop)

    @pl.when(is_last)
    def _():
        greet(near)
        greet(near + mid)
        greet(near + late)
        greet(far + last)

    loads[0].wait()
    for w in range(walkers):
        buf[r, :, w * nocc : (w + 1) * nocc] = orb_own[w]
    targets = 8 + jnp.where(is_source, 5, 0) + jnp.where(is_hop | is_mid | is_late | is_round, 1, 0)
    pl.semaphore_wait(barrier, targets)

    sends = []

    def send(src, dst, send_sem, recv_sem, target):
        copy = pltpu.make_async_remote_copy(
            src_ref=src, dst_ref=dst, send_sem=send_sem, recv_sem=recv_sem,
            device_id=target, device_id_type=MESH,
        )
        copy.start()
        sends.append(copy)
        return copy

    tiles = walkers * nocc // LANE
    top = (tiles + 1) // 2
    mid_a, mid_b = (top + 1) // 2, (top + tiles) // 2
    pieces = {
        "A": (0, top), "A1": (0, mid_a), "A2": (mid_a, top - mid_a),
        "B": (top, tiles - top), "B1": (top, mid_b - top), "B2": (mid_b, tiles - mid_b),
    }
    used = [0]

    def pass_on(origin, piece, target):
        i = used[0]
        used[0] += 1
        first, count = pieces[piece]
        ref = buf.at[origin, :, pl.ds(first * LANE, count * LANE)]
        return send(ref, ref, ag_send.at[i], ag_recv.at[i], target)

    def cut(i):
        return pl.ds(CUTS[i], CUTS[i + 1] - CUTS[i])

    def fac_copy(i, src, dst, send_sem, recv_sem, target):
        return pltpu.make_async_remote_copy(
            src_ref=src, dst_ref=dst, send_sem=send_sem, recv_sem=recv_sem,
            device_id=(target, r), device_id_type=MESH,
        )

    def vectors(first, count, i, ref):
        return ref.at[pl.ds(first, count), :, cut(i)]

    def several(i, src, dst, send_sem, recv_sems, target):
        def some(first, count, recv_sem):
            return fac_copy(
                i, vectors(first, count, i, src), vectors(first, count, i, dst), send_sem, recv_sem, target
            )

        step = vecs // len(recv_sems)
        whole = functools.partial(some, 0, vecs, recv_sems[0])
        return Several(whole, [some(k * step, step, sem) for k, sem in enumerate(recv_sems)])

    def direct(i):
        return several(i, fac, fac_in, fac_send.at[i], [fac_recv.at[i]], before)

    def first_leg(i, target):
        return several(i, fac, relay, fac_send.at[i], [relay_recv.at[k] for k in range(LEGS)], target)

    def last_leg(i, target):
        return several(i, relay, fac_in, relay_send.at[0], [fac_recv.at[i]] * LEGS, target)

    def next_leg(i, target):
        return several(i, relay, relay, relay_send.at[0], [relay_recv.at[k] for k in range(LEGS)], target)

    def hand_over(first, last):
        for here, there in zip(first.parts, last.parts):
            here.wait_recv()
            there.start()

    fac_copies = [direct(i) for i in range(len(CUTS) - 1)]
    to_here, from_here = first_leg(HERE, far), last_leg(HERE, near + turn - 1)
    to_round, from_round = first_leg(ROUND, near + last), last_leg(ROUND, far + turn - 1)
    to_hop, to_late, from_late = first_leg(LATE, near + hop), next_leg(LATE, far + late), last_leg(LATE, near + turn - 1)
    to_mid, from_mid = first_leg(MID, far + mid), last_leg(MID, near + turn - 1)

    rot_copy = send(rot, rot_in, rot_sem.at[0], rot_sem.at[1], (before, r))
    across_a, across_b = pass_on(r, "A", across), pass_on(r, "B", across)
    up_a, down_b = pass_on(r, "A", up), pass_on(r, "B", down)
    up_b, down_a = pass_on(r, "B", up), pass_on(r, "A", down)
    @pl.when(is_source)
    def _():
        to_round.start()
        to_hop.start()
        to_mid.start()

    def send_parts(*parts):
        @pl.when(jnp.logical_not(is_source))
        def _():
            for i in parts:
                fac_copies[i].start()

    send_parts(*ORDER[:2])

    loads[1].wait()
    loads[2].wait()
    part[0] = partial_bias(green_own, rot_own)
    bias[0, r] = part[0]
    for d in range(1, 8):
        send(part.at[0], bias.at[0, r], bias_send.at[0, d], bias_recv.at[0, r], (l, lax.rem(r + d, 8)))

    rot_copy.wait_recv()
    part[1] = partial_bias(green_own, rot_in)
    bias[1, r] = part[1]
    for d in range(1, 8):
        send(part.at[1], bias.at[1, r], bias_send.at[1, d], bias_recv.at[1, r], (l, lax.rem(r + d, 8)))
    out[...] = jnp.zeros_like(out)

    up_a.wait_recv()
    pass_2 = pass_on(row(0, 3), "A", up)
    down_b.wait_recv()
    pass_3 = pass_on(row(0, 1), "B", down)
    send_parts(ORDER[2])
    @pl.when(is_source)
    def _():
        to_here.start()

    @pl.when(is_round)
    def _():
        hand_over(to_round, from_round)

    @pl.when(is_hop)
    def _():
        hand_over(to_hop, to_late)

    across_b.wait_recv()
    pass_4p = pass_on(row(1, 0), "B1", up), pass_on(row(1, 0), "B2", up)
    across_a.wait_recv()
    pass_4m = pass_on(row(1, 0), "A1", down), pass_on(row(1, 0), "A2", down)

    send_parts(ORDER[3])
    pass_2x, pass_3x = pass_on(row(0, 3), "A", across), pass_on(row(0, 1), "B", across)

    @pl.when(is_source)
    def _():
        hand_over(to_here, from_here)

    @pl.when(is_mid)
    def _():
        hand_over(to_mid, from_mid)

    @pl.when(is_late)
    def _():
        hand_over(to_late, from_late)

    block = jnp.int32(0)
    for k in range(peers):
        block = jnp.where(start_pos[k] == l, jnp.int32(k), block)
    table = noise[block]
    columns = table.shape[1]
    row_id = lax.broadcasted_iota(jnp.int32, (columns, 2 * vecs * TILE), 0)
    col_id = lax.broadcasted_iota(jnp.int32, (columns, 2 * vecs * TILE), 1)
    pick = (row_id == lax.rem(l * vecs + col_id // TILE, columns)).astype(F32)
    noise_part = exact_dot(table, pick)

    for s in range(2):
        for d in range(1, 8):
            j = lax.rem(r + d, 8)
            pltpu.make_async_remote_copy(
                src_ref=part.at[s], dst_ref=bias.at[s, j], send_sem=bias_send.at[s, d],
                recv_sem=bias_recv.at[s, j], device_id=across, device_id_type=MESH,
            ).wait_recv()
    sums = []
    for s in range(2):
        total = bias[s, 0]
        for j in range(1, 8):
            total += bias[s, j]
        sums.append(total)
    shifted = (noise_part - jnp.concatenate(sums, axis=1)).astype(BF16).astype(F32)
    depth = 2 * vecs * TILE
    spread = jnp.broadcast_to(shifted[:, None, :], (walkers, TILE, depth)).reshape(walkers * TILE, depth)
    mix[...] = jnp.where(same_slot(walkers * TILE, depth, TILE), spread, 0.0).astype(BF16)
    whole = nrow // TILE
    left = nrow - whole * TILE
    if left:
        row_id = lax.broadcasted_iota(jnp.int32, (depth, 2 * vecs * left), 0)
        col_id = lax.broadcasted_iota(jnp.int32, (depth, 2 * vecs * left), 1)
        few = exact_dot(shifted, (row_id == col_id // left * TILE).astype(F32))
        spread = jnp.broadcast_to(few[:, None, :], (walkers, left, 2 * vecs * left))
        spread = spread.reshape(walkers * left, 2 * vecs * left)
        mix_left[...] = jnp.where(same_slot(walkers * left, 2 * vecs * left, left), spread, 0.0).astype(BF16)

    def operator_of(shard):
        lanes = slice(shard * nrow, (shard + 1) * nrow)

        @pl.loop(0, whole, unroll=whole)
        def _(block):
            rows = pl.ds(pl.multiple_of(block * TILE, TILE), TILE)
            both = jnp.concatenate(
                [f[:, rows, lanes].reshape(vecs * TILE, nrow) for f in (fac_own, fac_in)], axis=0
            )
            result = jnp.dot(mix[...], both, preferred_element_type=F32).astype(BF16)
            oper[shard, :, rows, :] = result.reshape(walkers, TILE, nrow)

        if left:
            rows = slice(whole * TILE, nrow)
            both = jnp.concatenate(
                [f[:, rows, lanes].astype(F32).reshape(vecs * left, nrow) for f in (fac_own, fac_in)], axis=0
            ).astype(BF16)
            result = jnp.dot(mix_left[...], both, preferred_element_type=F32)
            oper[shard, :, rows, :] = result.reshape(walkers, left, nrow).astype(BF16)

    def apply(shards):
        for w in range(walkers):
            lanes = slice(w * nocc, (w + 1) * nocc)
            total = out[w]
            for shard in shards:
                total += jnp.dot(oper[shard, w], buf[shard, :, lanes], preferred_element_type=F32)
            out[w] = total

    for copy in (up_b, down_a, pass_2, pass_3):
        copy.wait_recv()
    loads[3].wait()
    seen = [False] * len(ORDER)
    done = set()
    for i in ORDER:
        if i == ORDER[2]:
            final = []
            for n in range(2):
                pass_4p[n].wait_recv()
                final.append(pass_on(row(1, 3), ("B1", "B2")[n], up))
                pass_4m[n].wait_recv()
                final.append(pass_on(row(1, 1), ("A1", "A2")[n], down))
        fac_copies[i].wait_recv()
        seen[i] = True
        ready = []
        for shard in range(8):
            parts = [k for k in range(len(ORDER)) if CUTS[k] < (shard + 1) * nrow and CUTS[k + 1] > shard * nrow]
            if shard not in done and all(seen[k] for k in parts):
                ready.append(shard)
                operator_of(shard)
        done.update(ready)

        @pl.loop(ready[0], ready[-1] + 1)
        def _(shard):
            along = lax.rem(shard % 4 - y + 4, 4)
            early = (shard // 4 == half) | (along == 0)

            @pl.when(early)
            def _():
                apply((shard,))

    for copy in (pass_2x, pass_3x):
        copy.wait_recv()
    apply((row(1, 1), row(1, 3)))
    for copy in final:
        copy.wait_recv()
    apply((row(1, 2),))
    for copy in sends:
        copy.wait_send()
    for copy in fac_copies:
        copy.wait_send()

    @pl.when(is_source)
    def _():
        from_here.wait_send()

    @pl.when(is_round)
    def _():
        from_round.wait_send()

    @pl.when(is_hop)
    def _():
        to_late.wait_send()

    @pl.when(is_late)
    def _():
        from_late.wait_send()

    @pl.when(is_mid)
    def _():
        from_mid.wait_send()


def body(start_pos, field_noise, green_half, orbitals, rotated, factors):
    peers = lax.axis_size("loop")
    walkers, nrow, nocc = orbitals.shape
    vecs, _, norb = factors.shape
    width = green_half.shape[2]
    left = nrow % TILE
    dma = pltpu.SemaphoreType.DMA
    vmem, hbm = pl.BlockSpec(memory_space=pltpu.VMEM), pl.BlockSpec(memory_space=pl.ANY)
    return pl.pallas_call(
        functools.partial(kernel, peers),
        out_shape=jax.ShapeDtypeStruct((walkers, nrow, nocc), F32),
        in_specs=[pl.BlockSpec(memory_space=pltpu.SMEM), vmem, hbm, hbm, hbm, hbm],
        out_specs=vmem,
        scratch_shapes=[
            pltpu.VMEM((8, nrow, walkers * nocc), BF16),
            pltpu.VMEM((walkers, nrow, nocc), BF16),
            pltpu.VMEM((walkers, nocc, width), BF16),
            pltpu.VMEM((vecs, nocc, width), BF16),
            pltpu.VMEM((vecs, nocc, width), BF16),
            pltpu.VMEM((vecs, nrow, norb), BF16),
            pltpu.VMEM((vecs, nrow, norb), BF16),
            pltpu.VMEM((vecs, nrow, norb), BF16),
            pltpu.VMEM((8, walkers, nrow, nrow), BF16),
            pltpu.VMEM((walkers * TILE, 2 * vecs * TILE), BF16),
            pltpu.VMEM((walkers * left, 2 * vecs * left), BF16),
            pltpu.VMEM((2, walkers, LANE), F32),
            pltpu.VMEM((2, 8, walkers, LANE), F32),
            dma((4,)),
            dma((18,)),
            dma((18,)),
            dma((len(ORDER),)),
            dma((len(ORDER),)),
            dma((1,)),
            dma((LEGS,)),
            dma((2,)),
            dma((2, 8)),
            dma((2, 8)),
        ],
        compiler_params=pltpu.CompilerParams(
            collective_id=0, has_side_effects=True, vmem_limit_bytes=60 * 2**20
        ),
        cost_estimate=pl.CostEstimate(
            flops=8 * walkers * nrow * norb * nocc, bytes_accessed=2 * 10**7, transcendentals=0
        ),
    )(start_pos, field_noise, green_half, orbitals, rotated, factors)


def solution(mesh):
    return jax.shard_map(
        body,
        mesh=mesh,
        in_specs=(
            P(),
            P(),
            P("loop", None, "row"),
            P("loop", "row", None),
            P("loop", None, "row"),
            P("loop", "row", None),
        ),
        out_specs=P("loop", "row", None),
        check_vma=False,
    )
```
